32 devices in a mesh: shard: 2 (over x), ctx: 4 (over y, core), tp: 4 (over z).
Axes of the slice: x: 2, y: 2, z: 4, core: 2. Of those that a mesh axis runs over, the one named last changes fastest.
Arguments:
- inputs: bfloat16 [4, 1536, 768], P('shard', 'ctx'), may hold values from -6 to 6
- cotangent: bfloat16 [4, 1536, 768], P('shard', 'ctx'), may hold values from -6 to 6
- ln1_gain: float32 [768], replicated, may hold values from 0.25 to 1.75
- ln1_bias: float32 [768], replicated, may hold values from -4 to 4
- w_qkv: bfloat16 [3, 768, 768], P(None, 'shard', 'tp'), may hold values from -0.21875 to 0.21875
- q_bias: float32 [768], P('tp'), may hold values from -6 to 6
- v_bias: float32 [768], P('tp'), may hold values from -1.5 to 1.5
- w_out: bfloat16 [768, 768], P('tp', 'shard'), may hold values from -2.5 to 2.5
- out_bias: float32 [768], replicated, may hold values from -4 to 4
- ln2_gain: float32 [768], replicated, may hold values from 0.25 to 1.75
- ln2_bias: float32 [768], replicated, may hold values from -4 to 4
- w_up: bfloat16 [768, 3072], P('shard', 'tp'), may hold values from -0.21875 to 0.21875
- up_bias: float32 [3072], P('tp'), may hold values from -6 to 6
- w_down: bfloat16 [3072, 768], P('tp', 'shard'), may hold values from -0.109375 to 0.109375
- down_bias: float32 [768], replicated, may hold values from -4 to 4
Outputs:
- output: bfloat16 [4, 1536, 768], P('shard', 'ctx')
- grad_inputs: bfloat16 [4, 1536, 768], P('shard', 'ctx')
- grad_ln1_gain: float32 [768], replicated
- grad_ln1_bias: float32 [768], replicated
- grad_qkv: float32 [3, 768, 768], P(None, 'shard', 'tp')
- grad_q_bias: float32 [768], P('tp')
- grad_v_bias: float32 [768], P('tp')
- grad_w_out: float32 [768, 768], P('tp', 'shard')
- grad_out_bias: float32 [768], replicated
- grad_ln2_gain: float32 [768], replicated
- grad_ln2_bias: float32 [768], replicated
- grad_w_up: float32 [768, 3072], P('shard', 'tp')
- grad_up_bias: float32 [3072], P('tp')
- grad_w_down: float32 [3072, 768], P('tp', 'shard')
- grad_down_bias: float32 [768], replicated
The draws below stay inside these ranges and needn't reach their ends.
All inputs are finite; a program needn't handle non-finite values.
Results may differ from the reference program's by a relative error of at most 0.02.
Values may be sent and summed in bfloat16 or wider, within the bound.
A program may use at most 128 MiB of HBM per device.

```python
import jax
import jax.numpy as jnp
from jax import lax

D = 768
HEADS = 12
HEAD_DIM = 64
FF = 3072
FRAMES = 1536
CLIPS = 4


def levels(key, shape, pieces, low, top_value):
    gain, own = 1.0, jax.random.fold_in(key, 6)
    for dim, parts in pieces:
        heights = jnp.exp(jax.random.uniform(jax.random.fold_in(own, dim), (parts,), jnp.float32, low / len(pieces), top_value / len(pieces)))
        gain = gain * jnp.repeat(heights, shape[dim] // parts).reshape([-1 if axis == dim else 1 for axis in range(len(shape))])
    return gain


def gaussian(own_key, dims, spread, limit, split=(), dtype=jnp.bfloat16):
    drawn = jax.random.normal(own_key, dims, jnp.float32) * spread
    if len(split) > 0:
        drawn = levels(own_key, dims, split, -0.22, 0.18) * drawn
    return jnp.clip(drawn, min=-limit, max=limit).astype(dtype)


def setup_inputs(seed: int = 0) -> dict:
    key_list = jax.random.split(jax.random.key(seed), 16)
    return {
        "inputs": gaussian(key_list[0], (CLIPS, FRAMES, D), 1.0, 6.0, ((0, 2), (1, 4))),
        "cotangent": gaussian(key_list[1], (CLIPS, FRAMES, D), 1.0, 6.0, ((0, 2), (1, 4))),
        "ln1_gain": jnp.clip(1.0 + 0.15 * jax.random.normal(key_list[2], (D,), jnp.float32), 0.25, 1.75),
        "ln1_bias": gaussian(key_list[3], (D,), 0.3, 4.0, (), jnp.float32),
        "w_qkv": gaussian(key_list[4], (3, D, D), D ** -0.5, 0.21875, ((1, 2), (2, 4))),
        "q_bias": gaussian(key_list[5], (D,), 0.5, 6.0, ((0, 4),), jnp.float32),
        "v_bias": gaussian(key_list[6], (D,), 0.1, 1.5, ((0, 4),), jnp.float32),
        "w_out": gaussian(key_list[7], (D, D), (max(D // 128, 1)) ** -0.5, 2.5, ((0, 4), (1, 2))),
        "out_bias": gaussian(key_list[8], (D,), 0.3, 4.0, (), jnp.float32),
        "ln2_gain": jnp.clip(1.0 + 0.15 * jax.random.normal(key_list[9], (D,), jnp.float32), 0.25, 1.75),
        "ln2_bias": gaussian(key_list[10], (D,), 0.3, 4.0, (), jnp.float32),
        "w_up": gaussian(key_list[11], (D, FF), D ** -0.5, 0.21875, ((0, 2), (1, 4))),
        "up_bias": gaussian(key_list[12], (FF,), 0.5, 6.0, ((0, 4),), jnp.float32),
        "w_down": gaussian(key_list[13], (FF, D), FF ** -0.5, 0.109375, ((0, 4), (1, 2))),
        "down_bias": gaussian(key_list[14], (D,), 0.3, 4.0, (), jnp.float32),
    }


@jax.custom_vjp
def low(v):
    return lax.optimization_barrier(v.astype(jnp.bfloat16)).astype(jnp.float32)

@jax.custom_vjp
def low_back(v):
    return v

def low_keep(v):
    return (low(v), None)

def low_pass(kept, grad):
    return (grad,)

def back_keep(v):
    return (v, None)

def back_low(kept, grad):
    return (low(grad),)
low.defvjp(low_keep, low_pass)
low_back.defvjp(back_keep, back_low)
norm_eps = 1e-05

def norm_rows(inputs_f, gain_vec, bias_vec):
    row_mean = lax.optimization_barrier(jnp.mean(inputs_f, -1, keepdims=True))
    centred = inputs_f - row_mean
    row_var = lax.optimization_barrier(jnp.mean(centred * centred, -1, keepdims=True))
    return centred * lax.rsqrt(row_var + norm_eps) * gain_vec + bias_vec

def matmul(left, right):
    return jnp.dot(left, right, precision=lax.Precision.HIGHEST)

def clip_layer(clip_rows, weight_set):
    ln1_gain, ln1_bias, w_qkv, q_bias, v_bias, w_out, out_bias, ln2_gain, ln2_bias, w_up, up_bias, w_down, down_bias = weight_set
    frame_count = clip_rows.shape[0]
    act_one = low(norm_rows(clip_rows, ln1_gain, ln1_bias))
    queries = low(low_back(matmul(act_one, w_qkv[0]) + q_bias))
    key_rows = low(low_back(matmul(act_one, w_qkv[1])))
    value_rows = low(low_back(matmul(act_one, w_qkv[2]) + v_bias))
    q_heads = queries.reshape(frame_count, HEADS, HEAD_DIM)
    k_heads = key_rows.reshape(frame_count, HEADS, HEAD_DIM)
    v_heads = value_rows.reshape(frame_count, HEADS, HEAD_DIM)
    scores = jnp.einsum('qhe,khe->hqk', q_heads, k_heads, precision=lax.Precision.HIGHEST) * HEAD_DIM ** (-0.5)
    scores = low_back(scores)
    probs = jax.nn.softmax(scores, axis=-1)
    attended = jnp.einsum('hqk,khe->qhe', low(probs), v_heads, precision=lax.Precision.HIGHEST)
    attended = low(low_back(attended.reshape(frame_count, HEADS * HEAD_DIM)))
    mixed = low_back(matmul(attended, w_out))
    residual = clip_rows + mixed + out_bias
    act_two = low(norm_rows(residual, ln2_gain, ln2_bias))
    hidden_pre = low_back(matmul(act_two, w_up) + up_bias)
    hidden = low(jax.nn.gelu(hidden_pre, approximate=False))
    branch = low_back(matmul(hidden, w_down))
    return residual + branch + down_bias

def forward(inputs_f, weight_set):
    return lax.map(jax.checkpoint(lambda clip_rows: clip_layer(clip_rows, weight_set)), inputs_f)

def reference(inputs, cotangent, ln1_gain, ln1_bias, w_qkv, q_bias, v_bias, w_out, out_bias, ln2_gain, ln2_bias, w_up, up_bias, w_down, down_bias):
    weight_set = (ln1_gain.astype(jnp.float32), ln1_bias.astype(jnp.float32), w_qkv.astype(jnp.float32), q_bias.astype(jnp.float32), v_bias.astype(jnp.float32), w_out.astype(jnp.float32), out_bias.astype(jnp.float32), ln2_gain.astype(jnp.float32), ln2_bias.astype(jnp.float32), w_up.astype(jnp.float32), up_bias.astype(jnp.float32), w_down.astype(jnp.float32), down_bias.astype(jnp.float32))
    result, pullback = jax.vjp(forward, inputs.astype(jnp.float32), weight_set)
    grad_in, grad_set = pullback(cotangent.astype(jnp.float32))
    return (result.astype(jnp.bfloat16), grad_in.astype(jnp.bfloat16), grad_set[0], grad_set[1], grad_set[2], grad_set[3], grad_set[4], grad_set[5], grad_set[6], grad_set[7], grad_set[8], grad_set[9], grad_set[10], grad_set[11], grad_set[12])
```

```python
import functools

import jax
import jax.numpy as jnp
from jax import lax
from jax.experimental import pallas as pl
from jax.experimental.pallas import tpu as pltpu
from jax.sharding import PartitionSpec as P

HEAD_DIM = 64


norm_eps = 1e-05
inv_root_two = 0.7071067811865476
inv_root_tau = 0.3989422804014327


def norm_rows(inputs_f, gain_vec, bias_vec):
    row_mean = jnp.mean(inputs_f, -1, keepdims=True)
    centred = inputs_f - row_mean
    row_var = jnp.mean(centred * centred, -1, keepdims=True)
    inv_std = lax.rsqrt(row_var + norm_eps)
    unit_rows = centred * inv_std
    return (unit_rows * gain_vec + bias_vec, unit_rows, inv_std)


def norm_back(upstream, unit_rows, inv_std, gain_vec):
    scaled = upstream * gain_vec
    inner = (
        scaled
        - jnp.mean(scaled, -1, keepdims=True)
        - unit_rows * jnp.mean(scaled * unit_rows, -1, keepdims=True)
    )
    return inv_std * inner


def gelu_slope(pre_act):
    cumulative = 0.5 * (1.0 + lax.erf(pre_act * inv_root_two))
    density = jnp.exp(-0.5 * pre_act * pre_act) * inv_root_tau
    return cumulative + pre_act * density


MESH = pl.DeviceIdType.MESH
ROW_DIMS = (((0,), (0,)), ((), ()))
LAST_DIMS = (((1,), (1,)), ((), ()))
VMEM_BYTES = 50 * 1024 * 1024


def scores_of(q_ref, kv_ref, head, width):
    cols = slice(head * HEAD_DIM, (head + 1) * HEAD_DIM)
    vcols = slice(width + head * HEAD_DIM, width + (head + 1) * HEAD_DIM)
    blocks, _, block_len, _ = kv_ref.shape
    q = q_ref[0, :, cols] * jnp.bfloat16(HEAD_DIM**-0.5)
    k = kv_ref[:, 0, :, cols].reshape(blocks * block_len, HEAD_DIM)
    v = kv_ref[:, 0, :, vcols].reshape(blocks * block_len, HEAD_DIM)
    s = lax.dot_general(k, q, LAST_DIMS, preferred_element_type=jnp.float32)
    return q, k, v, s


def attend_kernel(q_ref, kv_ref, o_ref, ot_ref, lse_ref):
    width = q_ref.shape[2]
    for head in range(width // HEAD_DIM):
        q, k, v, s = scores_of(q_ref, kv_ref, head, width)
        top = jnp.max(s, 0, keepdims=True)
        e = jnp.exp(s - top)
        total = jnp.sum(e, 0, keepdims=True)
        ot = lax.dot_general(
            v, e.astype(jnp.bfloat16), ROW_DIMS, preferred_element_type=jnp.float32
        )
        ot_ref[0, head * HEAD_DIM : (head + 1) * HEAD_DIM, :] = ot / total
        lse_ref[0, head : head + 1, :] = top + jnp.log(total)
    o_ref[0] = ot_ref[0].T.astype(jnp.bfloat16)


def attend(q, kv):
    clips, length, width = q.shape
    blocks = kv.shape[0]
    heads = width // HEAD_DIM
    work = clips * heads * length * blocks * length
    row = pl.BlockSpec((1, length, width), lambda c: (c, 0, 0))
    return pl.pallas_call(
        attend_kernel,
        grid=(clips,),
        in_specs=[row, pl.BlockSpec((blocks, 1, length, 2 * width), lambda c: (0, c, 0, 0))],
        out_specs=[
            row,
            pl.BlockSpec((1, width, length), lambda c: (c, 0, 0)),
            pl.BlockSpec((1, 8, length), lambda c: (c, 0, 0)),
        ],
        out_shape=[
            jax.ShapeDtypeStruct(q.shape, jnp.bfloat16),
            jax.ShapeDtypeStruct((clips, width, length), jnp.float32),
            jax.ShapeDtypeStruct((clips, 8, length), jnp.float32),
        ],
        compiler_params=pltpu.CompilerParams(vmem_limit_bytes=VMEM_BYTES),
        cost_estimate=pl.CostEstimate(
            flops=4 * work * HEAD_DIM, bytes_accessed=4 * q.size * 5, transcendentals=work
        ),
    )(q, kv)


def attend_back_kernel(q_ref, kv_ref, do_ref, ot_ref, lse_ref, dq_ref, dkv_ref, dqt_ref):
    width = q_ref.shape[2]
    blocks, _, block_len, _ = kv_ref.shape
    scale = HEAD_DIM**-0.5
    dot_all = do_ref[0].astype(jnp.float32).T
    for head in range(width // HEAD_DIM):
        cols = slice(head * HEAD_DIM, (head + 1) * HEAD_DIM)
        vcols = slice(width + head * HEAD_DIM, width + (head + 1) * HEAD_DIM)
        q, k, v, s = scores_of(q_ref, kv_ref, head, width)
        do = do_ref[0, :, cols]
        delta = jnp.sum(dot_all[cols, :] * ot_ref[0, cols, :], 0, keepdims=True)
        p = jnp.exp(s - lse_ref[0, head : head + 1, :])
        dp = lax.dot_general(v, do, LAST_DIMS, preferred_element_type=jnp.float32)
        ds = (p * (dp - delta)).astype(jnp.bfloat16)
        dv = jnp.dot(p.astype(jnp.bfloat16), do, preferred_element_type=jnp.float32)
        dk = jnp.dot(ds, q, preferred_element_type=jnp.float32)
        dqt_ref[cols, :] = (
            lax.dot_general(k, ds, ROW_DIMS, preferred_element_type=jnp.float32) * scale
        )
        dkv_ref[:, 0, :, cols] = dk.astype(jnp.bfloat16).reshape(blocks, block_len, HEAD_DIM)
        dkv_ref[:, 0, :, vcols] = dv.astype(jnp.bfloat16).reshape(blocks, block_len, HEAD_DIM)
    dq_ref[0] = dqt_ref[...].T.astype(jnp.bfloat16)


def attend_back(q, kv, do, ot, lse):
    clips, length, width = q.shape
    blocks = kv.shape[0]
    heads = width // HEAD_DIM
    work = clips * heads * length * blocks * length
    row = pl.BlockSpec((1, length, width), lambda c: (c, 0, 0))
    wide = pl.BlockSpec((blocks, 1, length, 2 * width), lambda c: (0, c, 0, 0))
    return pl.pallas_call(
        attend_back_kernel,
        grid=(clips,),
        in_specs=[
            row,
            wide,
            row,
            pl.BlockSpec((1, width, length), lambda c: (c, 0, 0)),
            pl.BlockSpec((1, 8, length), lambda c: (c, 0, 0)),
        ],
        out_specs=[row, wide],
        out_shape=[
            jax.ShapeDtypeStruct(q.shape, jnp.bfloat16),
            jax.ShapeDtypeStruct(kv.shape, jnp.bfloat16),
        ],
        scratch_shapes=[pltpu.VMEM((width, length), jnp.float32)],
        compiler_params=pltpu.CompilerParams(vmem_limit_bytes=VMEM_BYTES),
        cost_estimate=pl.CostEstimate(
            flops=10 * work * HEAD_DIM, bytes_accessed=4 * q.size * 10, transcendentals=work
        ),
    )(q, kv, do, ot, lse)


def greet(partners):
    barrier = pltpu.get_barrier_semaphore()
    for partner in partners:
        pl.semaphore_signal(barrier, inc=1, device_id=partner, device_id_type=MESH)
    pl.semaphore_wait(barrier, len(partners))


def remote(src, dst, sems, slot, partner):
    copy = pltpu.make_async_remote_copy(
        src_ref=src,
        dst_ref=dst,
        send_sem=sems[0].at[slot],
        recv_sem=sems[1].at[slot],
        device_id=partner,
        device_id_type=MESH,
    )
    copy.start()
    return copy


def owner_sums_kernel(count, *refs):
    parts, outs, rest = refs[:count], refs[count : 2 * count], refs[2 * count :]
    per = 7
    scratch = [rest[per * i : per * (i + 1)] for i in range(count)]
    sems = rest[per * count :]
    shard, ctx, tp = lax.axis_index("shard"), lax.axis_index("ctx"), lax.axis_index("tp")
    side, core = ctx // 2, ctx % 2
    by_core = (shard, side * 2 + 1 - core, tp)
    by_shard = (1 - shard, ctx, tp)
    by_side = (shard, (1 - side) * 2 + core, tp)
    greet((by_core, by_shard, by_side))
    first = [
        remote(parts[i].at[1 - core], scratch[i][0], sems, 4 * i, by_core) for i in range(count)
    ]
    second, third, fourth = [], [], []
    for i in range(count):
        in_one, send_two, in_two, send_three, in_three, send_four, in_four = scratch[i]
        first[i].wait()
        send_two[...] = (
            parts[i][core, 1 - shard].astype(jnp.float32)
            + in_one[1 - shard].astype(jnp.float32)
        ).astype(jnp.bfloat16)
        second.append(remote(send_two, in_two, sems, 4 * i + 1, by_shard))
    for i in range(count):
        in_one, send_two, in_two, send_three, in_three, send_four, in_four = scratch[i]
        second[i].wait()
        send_three[...] = (
            parts[i][core, shard].astype(jnp.float32)
            + in_one[shard].astype(jnp.float32)
            + in_two[...].astype(jnp.float32)
        ).astype(jnp.bfloat16)
        third.append(remote(send_three, in_three, sems, 4 * i + 2, by_side))
    for i in range(count):
        in_one, send_two, in_two, send_three, in_three, send_four, in_four = scratch[i]
        third[i].wait()
        send_four[...] = (
            send_three[...].astype(jnp.float32) + in_three[...].astype(jnp.float32)
        ).astype(jnp.bfloat16)
        fourth.append(remote(send_four, in_four, sems, 4 * i + 3, by_core))
        outs[i][core] = send_four[...].astype(jnp.float32)
    for i in range(count):
        fourth[i].wait()
        outs[i][1 - core] = scratch[i][6][...].astype(jnp.float32)


def owner_sums(parts, collective):
    scratch = []
    for part in parts:
        piece = pltpu.VMEM(part.shape[2:], jnp.bfloat16)
        scratch += [pltpu.VMEM(part.shape[1:], jnp.bfloat16)] + [piece] * 6
    count = len(parts)
    size = sum(part.size for part in parts)
    vmem = pl.BlockSpec(memory_space=pltpu.VMEM)
    return pl.pallas_call(
        functools.partial(owner_sums_kernel, count),
        in_specs=[vmem] * count,
        out_specs=[vmem] * count,
        out_shape=[
            jax.ShapeDtypeStruct((part.shape[0],) + part.shape[2:], jnp.float32) for part in parts
        ],
        scratch_shapes=scratch + [pltpu.SemaphoreType.DMA((4 * count,))] * 2,
        compiler_params=pltpu.CompilerParams(
            collective_id=collective, has_side_effects=True, vmem_limit_bytes=VMEM_BYTES
        ),
        cost_estimate=pl.CostEstimate(flops=size, bytes_accessed=size * 30, transcendentals=0),
    )(*parts)


def small_sums_kernel(rows_all, vec_ref, out_ref, plane_in, line_out, line_in, sems_a, sems_b):
    shard, ctx, tp = lax.axis_index("shard"), lax.axis_index("ctx"), lax.axis_index("tp")
    n_shard, n_ctx, n_tp = (lax.axis_size(a) for a in ("shard", "ctx", "tp"))
    plane = n_shard * n_ctx
    me = shard * n_ctx + ctx
    partners = []
    for step in range(1, plane):
        other = lax.rem(me + step, plane)
        partners.append((other // n_ctx, lax.rem(other, n_ctx), tp))
    lines = [(shard, ctx, lax.rem(tp + step, n_tp)) for step in range(1, n_tp)]
    greet(partners + lines)
    copies = [
        remote(vec_ref, plane_in.at[step], (sems_a.at[0], sems_a.at[1]), step, partners[step])
        for step in range(plane - 1)
    ]
    for copy in copies:
        copy.wait()
    total = jnp.zeros_like(vec_ref[...])
    for source in range(plane):
        gap = lax.rem(me - source + plane, plane)
        slot = jnp.maximum(gap - 1, 0)
        total += jnp.where(gap == 0, vec_ref[...], plane_in[slot])
    line_out[...] = total[:rows_all]
    copies = [
        remote(line_out, line_in.at[step], (sems_b.at[0], sems_b.at[1]), step, lines[step])
        for step in range(n_tp - 1)
    ]
    out_ref[rows_all:] = total[rows_all:]
    for copy in copies:
        copy.wait()
    total = jnp.zeros_like(line_out[...])
    for source in range(n_tp):
        gap = lax.rem(tp - source + n_tp, n_tp)
        slot = jnp.maximum(gap - 1, 0)
        total += jnp.where(gap == 0, line_out[...], line_in[slot])
    out_ref[:rows_all] = total


def small_sums(vec, rows_all):
    plane = lax.axis_size("shard") * lax.axis_size("ctx")
    n_tp = lax.axis_size("tp")
    vmem = pl.BlockSpec(memory_space=pltpu.VMEM)
    low = (rows_all, vec.shape[1])
    return pl.pallas_call(
        functools.partial(small_sums_kernel, rows_all),
        in_specs=[vmem],
        out_specs=vmem,
        out_shape=jax.ShapeDtypeStruct(vec.shape, jnp.float32),
        scratch_shapes=[
            pltpu.VMEM((plane - 1,) + vec.shape, jnp.float32),
            pltpu.VMEM(low, jnp.float32),
            pltpu.VMEM((n_tp - 1,) + low, jnp.float32),
            pltpu.SemaphoreType.DMA((2, plane - 1)),
            pltpu.SemaphoreType.DMA((2, n_tp - 1)),
        ],
        compiler_params=pltpu.CompilerParams(
            collective_id=7, has_side_effects=True, vmem_limit_bytes=VMEM_BYTES
        ),
        cost_estimate=pl.CostEstimate(flops=vec.size, bytes_accessed=vec.size * 40, transcendentals=0),
    )(vec)


def tp_total(values):
    return lax.psum(values.astype(jnp.bfloat16), "tp").astype(jnp.float32)


def weight_totals(grad_wqkv, grad_wout, grad_wup, grad_wdown):
    low = [g.astype(jnp.bfloat16) for g in (grad_wqkv, grad_wout, grad_wup, grad_wdown)]
    if lax.axis_size("shard") != 2 or lax.axis_size("ctx") != 4:
        return [
            lax.psum(
                lax.psum_scatter(g, "shard", scatter_dimension=dim, tiled=True), "ctx"
            ).astype(jnp.float32)
            for g, dim in zip(low, (1, 1, 0, 1))
        ]
    three, width, local = grad_wqkv.shape
    hidden = grad_wup.shape[1]
    half, quarter = width // 2, width // 4
    up = low[2].reshape(2, 2, quarter, hidden).transpose(1, 0, 2, 3)
    down = low[3].reshape(2, hidden // 2, 2, half).transpose(0, 2, 1, 3)
    up, down = owner_sums((up, down), 3)
    qkv = low[0].reshape(three, 2, 2, quarter, local).transpose(2, 1, 0, 3, 4)
    out = low[1].reshape(2, local // 2, 2, half).transpose(0, 2, 1, 3)
    qkv, out = owner_sums((qkv.reshape(2, 2, three * quarter, local), out), 4)
    qkv = qkv.reshape(2, three, quarter, local).transpose(1, 0, 2, 3).reshape(three, half, local)
    return [
        qkv,
        out.reshape(local, half),
        up.reshape(half, hidden),
        down.reshape(hidden, half),
    ]


def shards(
    inputs,
    cotangent,
    ln1_gain,
    ln1_bias,
    w_qkv,
    q_bias,
    v_bias,
    w_out,
    out_bias,
    ln2_gain,
    ln2_bias,
    w_up,
    up_bias,
    w_down,
    down_bias,
):
    clip_count, block_len, model_width = inputs.shape
    count_of_rows = clip_count * block_len
    share_rows = count_of_rows // lax.axis_size("tp")
    share_start = lax.axis_index("tp") * share_rows

    def rows_part(values):
        return lax.dynamic_slice_in_dim(values, share_start, share_rows, 0)

    wqkv_full, wout_full, wup_full, wdown_full = (
        lax.all_gather(w_qkv, "shard", axis=1, tiled=True),
        lax.all_gather(w_out, "shard", axis=1, tiled=True),
        lax.all_gather(w_up, "shard", axis=0, tiled=True),
        lax.all_gather(w_down, "shard", axis=1, tiled=True),
    )
    shard_local_width = wqkv_full.shape[2]
    x_rows = inputs.astype(jnp.float32).reshape(count_of_rows, model_width)
    normed_one, unit_one, inv_one = norm_rows(x_rows, ln1_gain, ln1_bias)
    act_one = normed_one.astype(jnp.bfloat16)
    projected = jnp.einsum("rd,kdc->krc", act_one, wqkv_full, preferred_element_type=jnp.float32)
    queries = (projected[0] + q_bias).astype(jnp.bfloat16)
    key_rows = projected[1].astype(jnp.bfloat16)
    value_rows = (projected[2] + v_bias).astype(jnp.bfloat16)
    q_blocks = queries.reshape(clip_count, block_len, shard_local_width)
    key_values = jnp.concatenate([key_rows, value_rows], -1)
    key_values = lax.all_gather(
        key_values.reshape(clip_count, block_len, 2 * shard_local_width), "ctx", axis=0
    )
    attn_blocks, attn_cols, log_norm = attend(q_blocks, key_values)
    attn_low = attn_blocks.reshape(count_of_rows, shard_local_width)
    attn_term = jnp.dot(attn_low, wout_full, preferred_element_type=jnp.float32)
    residual = x_rows + tp_total(attn_term) + out_bias
    normed_two, unit_two, inv_two = norm_rows(residual, ln2_gain, ln2_bias)
    act_two = normed_two.astype(jnp.bfloat16)
    hidden_pre = jnp.dot(act_two, wup_full, preferred_element_type=jnp.float32) + up_bias
    hidden = jax.nn.gelu(hidden_pre, approximate=False).astype(jnp.bfloat16)
    branch_term = jnp.dot(hidden, wdown_full, preferred_element_type=jnp.float32)
    grad_y = cotangent.astype(jnp.float32).reshape(count_of_rows, model_width)
    grad_db = jnp.sum(rows_part(grad_y), 0)
    grad_ylow = grad_y.astype(jnp.bfloat16)
    grad_wdown = jnp.einsum("rf,rd->fd", hidden, grad_ylow, preferred_element_type=jnp.float32)
    grad_hidden = jnp.einsum("rd,fd->rf", grad_ylow, wdown_full, preferred_element_type=jnp.float32)
    grad_pre = (grad_hidden * gelu_slope(hidden_pre)).astype(jnp.bfloat16)
    grad_ub = jnp.sum(grad_pre.astype(jnp.float32), 0)
    grad_wup = jnp.einsum("rd,rf->df", act_two, grad_pre, preferred_element_type=jnp.float32)
    acttwo_term = jnp.einsum("rf,df->rd", grad_pre, wup_full, preferred_element_type=jnp.float32)
    grad_acttwo = tp_total(acttwo_term)
    grad_acttwo, branch_term = lax.optimization_barrier((grad_acttwo, branch_term.astype(jnp.bfloat16)))
    branch_total = lax.psum(branch_term, "tp").astype(jnp.float32)
    output = (
        (residual + branch_total + down_bias)
        .astype(jnp.bfloat16)
        .reshape(clip_count, block_len, model_width)
    )
    grad_resid = grad_y + norm_back(grad_acttwo, unit_two, inv_two, ln2_gain)
    grad_g2 = jnp.sum(rows_part(grad_acttwo) * rows_part(unit_two), 0)
    grad_b2 = jnp.sum(rows_part(grad_acttwo), 0)
    grad_ob = jnp.sum(rows_part(grad_resid), 0)
    grad_mixed = grad_resid.astype(jnp.bfloat16)
    grad_wout = jnp.einsum("rc,rd->cd", attn_low, grad_mixed, preferred_element_type=jnp.float32)
    grad_attn = jnp.einsum(
        "rd,cd->rc", grad_mixed, wout_full, preferred_element_type=jnp.float32
    ).astype(jnp.bfloat16)
    grad_query, grad_kv = attend_back(
        q_blocks,
        key_values,
        grad_attn.reshape(clip_count, block_len, shard_local_width),
        attn_cols,
        log_norm,
    )
    key_value_totals = lax.psum_scatter(grad_kv, "ctx", scatter_dimension=0, tiled=False)
    key_value_totals = key_value_totals.reshape(count_of_rows, 2 * shard_local_width)
    query_gradient_partial = grad_query.reshape(count_of_rows, shard_local_width)
    key_gradient_partial = key_value_totals[:, :shard_local_width]
    value_gradient_partial = key_value_totals[:, shard_local_width:]
    three = (query_gradient_partial, key_gradient_partial, value_gradient_partial)
    grad_qb = jnp.sum(query_gradient_partial.astype(jnp.float32), 0)
    grad_vb = jnp.sum(value_gradient_partial.astype(jnp.float32), 0)
    grad_wqkv = jnp.stack(
        [jnp.einsum("rd,rc->dc", act_one, part, preferred_element_type=jnp.float32) for part in three]
    )
    actone_term = sum(
        jnp.einsum("rc,dc->rd", part, wqkv_full[i], preferred_element_type=jnp.float32)
        for i, part in enumerate(three)
    )
    actone_term, output = lax.optimization_barrier((actone_term, output))
    grad_actone = tp_total(actone_term)
    input_norm = norm_back(grad_actone, unit_one, inv_one, ln1_gain)
    grad_g1 = jnp.sum(rows_part(grad_actone) * rows_part(unit_one), 0)
    grad_b1 = jnp.sum(rows_part(grad_actone), 0)
    grad_inputs = (
        (grad_resid + input_norm).astype(jnp.bfloat16).reshape(clip_count, block_len, model_width)
    )
    owned = weight_totals(grad_wqkv, grad_wout, grad_wup, grad_wdown)
    norm_rows_six = jnp.stack([grad_g1, grad_b1, grad_ob, grad_g2, grad_b2, grad_db])
    hidden_width = grad_ub.shape[0]
    if hidden_width == model_width and 2 * shard_local_width <= model_width:
        pad = jnp.zeros((model_width - 2 * shard_local_width,), jnp.float32)
        packed = jnp.concatenate(
            [
                norm_rows_six,
                jnp.zeros((2, model_width), jnp.float32),
                grad_ub[None],
                jnp.concatenate([grad_qb, grad_vb, pad])[None],
                jnp.zeros((6, model_width), jnp.float32),
            ]
        )
        summed = small_sums(packed, 8)
        norm_sums = summed[:6]
        vectors = (
            summed[9, :shard_local_width],
            summed[9, shard_local_width : 2 * shard_local_width],
            summed[8],
        )
    else:
        vectors = lax.psum((grad_qb, grad_vb, grad_ub), ("shard", "ctx"))
        norm_sums = lax.psum(norm_rows_six, ("shard", "ctx", "tp"))
    return (
        output,
        grad_inputs,
        norm_sums[0],
        norm_sums[1],
        owned[0],
        vectors[0],
        vectors[1],
        owned[1],
        norm_sums[2],
        norm_sums[3],
        norm_sums[4],
        owned[2],
        vectors[2],
        owned[3],
        norm_sums[5],
    )


def solution(mesh):
    placed = (
        P("shard", "ctx", None),
        P("shard", "ctx", None),
        P(),
        P(),
        P(None, "shard", "tp"),
        P("tp"),
        P("tp"),
        P("tp", "shard"),
        P(),
        P(),
        P(),
        P("shard", "tp"),
        P("tp"),
        P("tp", "shard"),
        P(),
    )
    return jax.shard_map(
        shards,
        mesh=mesh,
        in_specs=placed,
        out_specs=(
            P("shard", "ctx", None),
            P("shard", "ctx", None),
            P(),
            P(),
            P(None, "shard", "tp"),
            P("tp"),
            P("tp"),
            P("tp", "shard"),
            P(),
            P(),
            P(),
            P("shard", "tp"),
            P("tp"),
            P("tp", "shard"),
            P(),
        ),
        check_vma=False,
    )
```

```python
import functools

import jax
import jax.numpy as jnp
from jax import lax
from jax.experimental import pallas as pl
from jax.experimental.pallas import tpu as pltpu
from jax.sharding import PartitionSpec as P

HEAD_DIM = 64


norm_eps = 1e-05
inv_root_two = 0.7071067811865476
inv_root_tau = 0.3989422804014327


def norm_rows(inputs_f, gain_vec, bias_vec):
    row_mean = jnp.mean(inputs_f, -1, keepdims=True)
    centred = inputs_f - row_mean
    row_var = jnp.mean(centred * centred, -1, keepdims=True)
    inv_std = lax.rsqrt(row_var + norm_eps)
    unit_rows = centred * inv_std
    return (unit_rows * gain_vec + bias_vec, unit_rows, inv_std)


def norm_back(upstream, unit_rows, inv_std, gain_vec):
    scaled = upstream * gain_vec
    inner = (
        scaled
        - jnp.mean(scaled, -1, keepdims=True)
        - unit_rows * jnp.mean(scaled * unit_rows, -1, keepdims=True)
    )
    return inv_std * inner


def gelu_slope(pre_act):
    cumulative = 0.5 * (1.0 + lax.erf(pre_act * inv_root_two))
    density = jnp.exp(-0.5 * pre_act * pre_act) * inv_root_tau
    return cumulative + pre_act * density


MESH = pl.DeviceIdType.MESH
ROW_DIMS = (((0,), (0,)), ((), ()))
LAST_DIMS = (((1,), (1,)), ((), ()))
VMEM_BYTES = 50 * 1024 * 1024


def scores_of(q_ref, kv_ref, head, width):
    cols = slice(head * HEAD_DIM, (head + 1) * HEAD_DIM)
    vcols = slice(width + head * HEAD_DIM, width + (head + 1) * HEAD_DIM)
    blocks, _, block_len, _ = kv_ref.shape
    q = q_ref[0, :, cols] * jnp.bfloat16(HEAD_DIM**-0.5)
    k = kv_ref[:, 0, :, cols].reshape(blocks * block_len, HEAD_DIM)
    v = kv_ref[:, 0, :, vcols].reshape(blocks * block_len, HEAD_DIM)
    s = lax.dot_general(k, q, LAST_DIMS, preferred_element_type=jnp.float32)
    return q, k, v, s


def attend_kernel(q_ref, kv_ref, o_ref, ot_ref, lse_ref):
    width = q_ref.shape[2]
    for head in range(width // HEAD_DIM):
        q, k, v, s = scores_of(q_ref, kv_ref, head, width)
        top = jnp.max(s, 0, keepdims=True)
        e = jnp.exp(s - top)
        total = jnp.sum(e, 0, keepdims=True)
        ot = lax.dot_general(
            v, e.astype(jnp.bfloat16), ROW_DIMS, preferred_element_type=jnp.float32
        )
        ot_ref[0, head * HEAD_DIM : (head + 1) * HEAD_DIM, :] = ot / total
        lse_ref[0, head : head + 1, :] = top + jnp.log(total)
    o_ref[0] = ot_ref[0].T.astype(jnp.bfloat16)


def attend(q, kv):
    clips, length, width = q.shape
    blocks = kv.shape[0]
    heads = width // HEAD_DIM
    work = clips * heads * length * blocks * length
    row = pl.BlockSpec((1, length, width), lambda c: (c, 0, 0))
    return pl.pallas_call(
        attend_kernel,
        grid=(clips,),
        in_specs=[row, pl.BlockSpec((blocks, 1, length, 2 * width), lambda c: (0, c, 0, 0))],
        out_specs=[
            row,
            pl.BlockSpec((1, width, length), lambda c: (c, 0, 0)),
            pl.BlockSpec((1, 8, length), lambda c: (c, 0, 0)),
        ],
        out_shape=[
            jax.ShapeDtypeStruct(q.shape, jnp.bfloat16),
            jax.ShapeDtypeStruct((clips, width, length), jnp.float32),
            jax.ShapeDtypeStruct((clips, 8, length), jnp.float32),
        ],
        compiler_params=pltpu.CompilerParams(vmem_limit_bytes=VMEM_BYTES),
        cost_estimate=pl.CostEstimate(
            flops=4 * work * HEAD_DIM, bytes_accessed=4 * q.size * 5, transcendentals=work
        ),
    )(q, kv)


def attend_back_kernel(q_ref, kv_ref, do_ref, ot_ref, lse_ref, dq_ref, dkv_ref, dqt_ref):
    width = q_ref.shape[2]
    blocks, _, block_len, _ = kv_ref.shape
    scale = HEAD_DIM**-0.5
    dot_all = do_ref[0].astype(jnp.float32).T
    for head in range(width // HEAD_DIM):
        cols = slice(head * HEAD_DIM, (head + 1) * HEAD_DIM)
        vcols = slice(width + head * HEAD_DIM, width + (head + 1) * HEAD_DIM)
        q, k, v, s = scores_of(q_ref, kv_ref, head, width)
        do = do_ref[0, :, cols]
        delta = jnp.sum(dot_all[cols, :] * ot_ref[0, cols, :], 0, keepdims=True)
        p = jnp.exp(s - lse_ref[0, head : head + 1, :])
        dp = lax.dot_general(v, do, LAST_DIMS, preferred_element_type=jnp.float32)
        ds = (p * (dp - delta)).astype(jnp.bfloat16)
        dv = jnp.dot(p.astype(jnp.bfloat16), do, preferred_element_type=jnp.float32)
        dk = jnp.dot(ds, q, preferred_element_type=jnp.float32)
        dqt_ref[cols, :] = (
            lax.dot_general(k, ds, ROW_DIMS, preferred_element_type=jnp.float32) * scale
        )
        dkv_ref[:, 0, :, cols] = dk.astype(jnp.bfloat16).reshape(blocks, block_len, HEAD_DIM)
        dkv_ref[:, 0, :, vcols] = dv.astype(jnp.bfloat16).reshape(blocks, block_len, HEAD_DIM)
    dq_ref[0] = dqt_ref[...].T.astype(jnp.bfloat16)


def attend_back(q, kv, do, ot, lse):
    clips, length, width = q.shape
    blocks = kv.shape[0]
    heads = width // HEAD_DIM
    work = clips * heads * length * blocks * length
    row = pl.BlockSpec((1, length, width), lambda c: (c, 0, 0))
    wide = pl.BlockSpec((blocks, 1, length, 2 * width), lambda c: (0, c, 0, 0))
    return pl.pallas_call(
        attend_back_kernel,
        grid=(clips,),
        in_specs=[
            row,
            wide,
            row,
            pl.BlockSpec((1, width, length), lambda c: (c, 0, 0)),
            pl.BlockSpec((1, 8, length), lambda c: (c, 0, 0)),
        ],
        out_specs=[row, wide],
        out_shape=[
            jax.ShapeDtypeStruct(q.shape, jnp.bfloat16),
            jax.ShapeDtypeStruct(kv.shape, jnp.bfloat16),
        ],
        scratch_shapes=[pltpu.VMEM((width, length), jnp.float32)],
        compiler_params=pltpu.CompilerParams(vmem_limit_bytes=VMEM_BYTES),
        cost_estimate=pl.CostEstimate(
            flops=10 * work * HEAD_DIM, bytes_accessed=4 * q.size * 10, transcendentals=work
        ),
    )(q, kv, do, ot, lse)


def greet(partners):
    barrier = pltpu.get_barrier_semaphore()
    for partner in partners:
        pl.semaphore_signal(barrier, inc=1, device_id=partner, device_id_type=MESH)
    pl.semaphore_wait(barrier, len(partners))


def remote(src, dst, sems, slot, partner):
    copy = pltpu.make_async_remote_copy(
        src_ref=src,
        dst_ref=dst,
        send_sem=sems[0].at[slot],
        recv_sem=sems[1].at[slot],
        device_id=partner,
        device_id_type=MESH,
    )
    copy.start()
    return copy


def places():
    shard, ctx, tp = lax.axis_index("shard"), lax.axis_index("ctx"), lax.axis_index("tp")
    side, core = ctx // 2, ctx % 2
    by_core = (shard, side * 2 + 1 - core, tp)
    by_shard = (1 - shard, ctx, tp)
    by_side = (shard, (1 - side) * 2 + core, tp)
    return shard, side, core, by_core, by_shard, by_side


def in_pairs():
    return lax.axis_size("shard") == 2 and lax.axis_size("ctx") == 4


def piece_of(ref, shard, core):
    if len(ref.shape) == 4:
        return ref.at[shard, core]
    half = ref.shape[2] // 2
    return ref.at[core, :, pl.ds(pl.multiple_of(shard * half, half), half)]


def piece_shape(part):
    if part.ndim == 4:
        return part.shape[2:]
    return (part.shape[1], part.shape[2] // 2)


def wide_f32(ref):
    return ref[...].astype(jnp.float32)


def owner_sums_kernel(count, *refs):
    parts, outs, rest = refs[:count], refs[count : 2 * count], refs[2 * count :]
    per = 7
    scratch = [rest[per * i : per * (i + 1)] for i in range(count)]
    sems = rest[per * count :]
    shard, side, core, by_core, by_shard, by_side = places()
    greet((by_core, by_shard, by_side))
    first = []
    for i in range(count):
        for slot, owner in enumerate((1 - shard, shard)):
            first.append(
                remote(
                    piece_of(parts[i], owner, 1 - core),
                    scratch[i][0].at[slot],
                    sems,
                    5 * i + slot,
                    by_core,
                )
            )
    second, third, fourth = [], [], []
    for i in range(count):
        in_one, send_two, in_two, send_three, in_three, send_four, in_four = scratch[i]
        first[2 * i].wait()
        send_two[...] = (
            wide_f32(piece_of(parts[i], 1 - shard, core)) + wide_f32(in_one.at[0])
        ).astype(jnp.bfloat16)
        second.append(remote(send_two, in_two, sems, 5 * i + 2, by_shard))
    for i in range(count):
        in_one, send_two, in_two, send_three, in_three, send_four, in_four = scratch[i]
        first[2 * i + 1].wait()
        second[i].wait()
        send_three[...] = (
            wide_f32(piece_of(parts[i], shard, core)) + wide_f32(in_one.at[1]) + wide_f32(in_two)
        ).astype(jnp.bfloat16)
        third.append(remote(send_three, in_three, sems, 5 * i + 3, by_side))
    for i in range(count):
        in_one, send_two, in_two, send_three, in_three, send_four, in_four = scratch[i]
        third[i].wait()
        send_four[...] = (wide_f32(send_three) + wide_f32(in_three)).astype(jnp.bfloat16)
        fourth.append(remote(send_four, in_four, sems, 5 * i + 4, by_core))
        outs[i][core] = wide_f32(send_four)
    for i in range(count):
        fourth[i].wait()
        outs[i][1 - core] = wide_f32(scratch[i][6])


def owner_sums(parts, collective):
    scratch = []
    for part in parts:
        shape = piece_shape(part)
        scratch += [pltpu.VMEM((2,) + shape, jnp.bfloat16)]
        scratch += [pltpu.VMEM(shape, jnp.bfloat16)] * 6
    count = len(parts)
    size = sum(part.size for part in parts)
    vmem = pl.BlockSpec(memory_space=pltpu.VMEM)
    return pl.pallas_call(
        functools.partial(owner_sums_kernel, count),
        in_specs=[vmem] * count,
        out_specs=[vmem] * count,
        out_shape=[jax.ShapeDtypeStruct((2,) + piece_shape(part), jnp.float32) for part in parts],
        scratch_shapes=scratch + [pltpu.SemaphoreType.DMA((5 * count,))] * 2,
        compiler_params=pltpu.CompilerParams(
            collective_id=collective, has_side_effects=True, vmem_limit_bytes=VMEM_BYTES
        ),
        cost_estimate=pl.CostEstimate(flops=size, bytes_accessed=size * 30, transcendentals=0),
    )(*parts)


def kv_gather_kernel(own_ref, all_ref, send_sem, recv_sem):
    shard, side, core, by_core, by_shard, by_side = places()
    clips = own_ref.shape[0]
    sems = (send_sem, recv_sem)
    mine, across = side * 2 + core, (1 - side) * 2 + core
    greet((by_core, by_side))
    sent = [
        remote(own_ref.at[c], all_ref.at[mine, c], sems, c, by_side) for c in range(clips)
    ]
    near = remote(own_ref, all_ref.at[mine], sems, 2 * clips, by_core)
    all_ref[mine] = own_ref[...]
    passed = []
    for c in range(clips):
        sent[c].wait()
        passed.append(
            remote(all_ref.at[across, c], all_ref.at[across, c], sems, clips + c, by_core)
        )
    near.wait()
    for copy in passed:
        copy.wait()


def kv_gather(own):
    if not in_pairs():
        return lax.all_gather(own, "ctx", axis=0)
    vmem = pl.BlockSpec(memory_space=pltpu.VMEM)
    return pl.pallas_call(
        kv_gather_kernel,
        in_specs=[vmem],
        out_specs=vmem,
        out_shape=jax.ShapeDtypeStruct((4,) + own.shape, own.dtype),
        scratch_shapes=[pltpu.SemaphoreType.DMA((2 * own.shape[0] + 1,))] * 2,
        compiler_params=pltpu.CompilerParams(
            collective_id=8, has_side_effects=True, vmem_limit_bytes=VMEM_BYTES
        ),
        cost_estimate=pl.CostEstimate(flops=0, bytes_accessed=own.size * 80, transcendentals=0),
    )(own)


def kv_scatter_kernel(all_ref, own_ref, in_core, send_side, in_side, send_sem, recv_sem):
    shard, side, core, by_core, by_shard, by_side = places()
    clips = own_ref.shape[0]
    sems = (send_sem, recv_sem)
    greet((by_core, by_side))
    near = [
        remote(
            all_ref.at[owner * 2 + 1 - core, c], in_core.at[slot, c], sems, slot * clips + c, by_core
        )
        for slot, owner in enumerate((1 - side, side))
        for c in range(clips)
    ]
    far = []
    for c in range(clips):
        near[c].wait()
        send_side[c] = (
            wide_f32(all_ref.at[(1 - side) * 2 + core, c]) + wide_f32(in_core.at[0, c])
        ).astype(jnp.bfloat16)
        far.append(remote(send_side.at[c], in_side.at[c], sems, 2 * clips + c, by_side))
    for c in range(clips):
        near[clips + c].wait()
        far[c].wait()
        own_ref[c] = (
            wide_f32(all_ref.at[side * 2 + core, c])
            + wide_f32(in_core.at[1, c])
            + wide_f32(in_side.at[c])
        ).astype(jnp.bfloat16)


def kv_scatter(parts):
    if not in_pairs():
        return lax.psum_scatter(parts, "ctx", scatter_dimension=0, tiled=False)
    vmem = pl.BlockSpec(memory_space=pltpu.VMEM)
    own = parts.shape[1:]
    return pl.pallas_call(
        kv_scatter_kernel,
        in_specs=[vmem],
        out_specs=vmem,
        out_shape=jax.ShapeDtypeStruct(own, parts.dtype),
        scratch_shapes=[
            pltpu.VMEM((2,) + own, jnp.bfloat16),
            pltpu.VMEM(own, jnp.bfloat16),
            pltpu.VMEM(own, jnp.bfloat16),
        ]
        + [pltpu.SemaphoreType.DMA((3 * own[0],))] * 2,
        compiler_params=pltpu.CompilerParams(
            collective_id=9, has_side_effects=True, vmem_limit_bytes=VMEM_BYTES
        ),
        cost_estimate=pl.CostEstimate(flops=0, bytes_accessed=parts.size * 25, transcendentals=0),
    )(parts)


def weight_gather_kernel(qkv_ref, out_ref, qkv_all, out_all, send_sem, recv_sem):
    shard, side, core, by_core, by_shard, by_side = places()
    sems = (send_sem, recv_sem)
    half, part = qkv_ref.shape[1] // 2, out_ref.shape[0] // 2
    cols = out_ref.shape[1]

    def qkv_slot(owner):
        return qkv_all.at[:, owner, pl.ds(pl.multiple_of(core * half, half), half), :]

    def out_slot(owner):
        return out_all.at[
            pl.ds(pl.multiple_of(core * part, part), part),
            pl.ds(pl.multiple_of(owner * cols, cols), cols),
        ]

    greet((by_core, by_shard))
    sent = [
        remote(
            qkv_ref.at[:, pl.ds(pl.multiple_of(core * half, half), half), :],
            qkv_slot(shard),
            sems,
            0,
            by_shard,
        ),
        remote(
            out_ref.at[pl.ds(pl.multiple_of(core * part, part), part), :],
            out_slot(shard),
            sems,
            1,
            by_shard,
        ),
    ]
    qkv_all[:, shard] = qkv_ref[...]
    out_all[:, pl.ds(pl.multiple_of(shard * cols, cols), cols)] = out_ref[...]
    sent[0].wait()
    passed = [remote(qkv_slot(1 - shard), qkv_slot(1 - shard), sems, 2, by_core)]
    sent[1].wait()
    passed.append(remote(out_slot(1 - shard), out_slot(1 - shard), sems, 3, by_core))
    for copy in passed:
        copy.wait()


def weight_gather(w_qkv, w_out):
    if not in_pairs():
        return (
            lax.all_gather(w_qkv, "shard", axis=1, tiled=True),
            lax.all_gather(w_out, "shard", axis=1, tiled=True),
        )
    three, rows, local = w_qkv.shape
    vmem = pl.BlockSpec(memory_space=pltpu.VMEM)
    qkv, out = pl.pallas_call(
        weight_gather_kernel,
        in_specs=[vmem, vmem],
        out_specs=[vmem, vmem],
        out_shape=[
            jax.ShapeDtypeStruct((three, 2, rows, local), w_qkv.dtype),
            jax.ShapeDtypeStruct((local, 2 * rows), w_out.dtype),
        ],
        scratch_shapes=[pltpu.SemaphoreType.DMA((4,))] * 2,
        compiler_params=pltpu.CompilerParams(
            collective_id=10, has_side_effects=True, vmem_limit_bytes=VMEM_BYTES
        ),
        cost_estimate=pl.CostEstimate(flops=0, bytes_accessed=w_qkv.size * 60, transcendentals=0),
    )(w_qkv, w_out)
    return qkv.reshape(three, 2 * rows, local), out


def small_sums_kernel(rows_all, vec_ref, out_ref, plane_in, line_out, line_in, sems_a, sems_b):
    shard, ctx, tp = lax.axis_index("shard"), lax.axis_index("ctx"), lax.axis_index("tp")
    n_shard, n_ctx, n_tp = (lax.axis_size(a) for a in ("shard", "ctx", "tp"))
    plane = n_shard * n_ctx
    me = shard * n_ctx + ctx
    partners = []
    for step in range(1, plane):
        other = lax.rem(me + step, plane)
        partners.append((other // n_ctx, lax.rem(other, n_ctx), tp))
    lines = [(shard, ctx, lax.rem(tp + step, n_tp)) for step in range(1, n_tp)]
    greet(partners + lines)
    copies = [
        remote(vec_ref, plane_in.at[step], (sems_a.at[0], sems_a.at[1]), step, partners[step])
        for step in range(plane - 1)
    ]
    for copy in copies:
        copy.wait()
    total = jnp.zeros_like(vec_ref[...])
    for source in range(plane):
        gap = lax.rem(me - source + plane, plane)
        slot = jnp.maximum(gap - 1, 0)
        total += jnp.where(gap == 0, vec_ref[...], plane_in[slot])
    line_out[...] = total[:rows_all]
    copies = [
        remote(line_out, line_in.at[step], (sems_b.at[0], sems_b.at[1]), step, lines[step])
        for step in range(n_tp - 1)
    ]
    out_ref[rows_all:] = total[rows_all:]
    for copy in copies:
        copy.wait()
    total = jnp.zeros_like(line_out[...])
    for source in range(n_tp):
        gap = lax.rem(tp - source + n_tp, n_tp)
        slot = jnp.maximum(gap - 1, 0)
        total += jnp.where(gap == 0, line_out[...], line_in[slot])
    out_ref[:rows_all] = total


def small_sums(vec, rows_all):
    plane = lax.axis_size("shard") * lax.axis_size("ctx")
    n_tp = lax.axis_size("tp")
    vmem = pl.BlockSpec(memory_space=pltpu.VMEM)
    low = (rows_all, vec.shape[1])
    return pl.pallas_call(
        functools.partial(small_sums_kernel, rows_all),
        in_specs=[vmem],
        out_specs=vmem,
        out_shape=jax.ShapeDtypeStruct(vec.shape, jnp.float32),
        scratch_shapes=[
            pltpu.VMEM((plane - 1,) + vec.shape, jnp.float32),
            pltpu.VMEM(low, jnp.float32),
            pltpu.VMEM((n_tp - 1,) + low, jnp.float32),
            pltpu.SemaphoreType.DMA((2, plane - 1)),
            pltpu.SemaphoreType.DMA((2, n_tp - 1)),
        ],
        compiler_params=pltpu.CompilerParams(
            collective_id=7, has_side_effects=True, vmem_limit_bytes=VMEM_BYTES
        ),
        cost_estimate=pl.CostEstimate(flops=vec.size, bytes_accessed=vec.size * 40, transcendentals=0),
    )(vec)


def tp_total(values):
    return lax.psum(values.astype(jnp.bfloat16), "tp").astype(jnp.float32)


def plain_totals(grad, dim):
    part = lax.psum_scatter(grad, "shard", scatter_dimension=dim, tiled=True)
    return lax.psum(part, "ctx").astype(jnp.float32)


def hidden_totals(grad_wup, grad_wdown):
    up, down = grad_wup.astype(jnp.bfloat16), grad_wdown.astype(jnp.bfloat16)
    if not in_pairs():
        return plain_totals(up, 0), plain_totals(down, 1)
    width, hidden = up.shape
    up, down = owner_sums(
        (up.reshape(2, 2, width // 4, hidden), down.reshape(2, hidden // 2, width)), 3
    )
    return up.reshape(width // 2, hidden), down.reshape(hidden, width // 2)


def mixer_totals(grad_three, grad_wout):
    three = [g.astype(jnp.bfloat16) for g in grad_three]
    out = grad_wout.astype(jnp.bfloat16)
    if not in_pairs():
        return plain_totals(jnp.stack(three), 1), plain_totals(out, 1)
    local, width = out.shape
    sums = owner_sums(
        tuple(g.reshape(2, 2, width // 4, local) for g in three)
        + (out.reshape(2, local // 2, width),),
        4,
    )
    qkv = jnp.stack([g.reshape(width // 2, local) for g in sums[:3]])
    return qkv, sums[3].reshape(local, width // 2)


def shards(
    inputs,
    cotangent,
    ln1_gain,
    ln1_bias,
    w_qkv,
    q_bias,
    v_bias,
    w_out,
    out_bias,
    ln2_gain,
    ln2_bias,
    w_up,
    up_bias,
    w_down,
    down_bias,
):
    clip_count, block_len, model_width = inputs.shape
    count_of_rows = clip_count * block_len
    share_rows = count_of_rows // lax.axis_size("tp")
    share_start = lax.axis_index("tp") * share_rows

    def rows_part(values):
        return lax.dynamic_slice_in_dim(values, share_start, share_rows, 0)

    wqkv_full, wout_full = weight_gather(w_qkv, w_out)
    wup_full, wdown_full = (
        lax.all_gather(w_up, "shard", axis=0, tiled=True),
        lax.all_gather(w_down, "shard", axis=1, tiled=True),
    )
    shard_local_width = wqkv_full.shape[2]
    x_rows = inputs.astype(jnp.float32).reshape(count_of_rows, model_width)
    normed_one, unit_one, inv_one = norm_rows(x_rows, ln1_gain, ln1_bias)
    act_one = normed_one.astype(jnp.bfloat16)
    projected = jnp.einsum("rd,kdc->krc", act_one, wqkv_full, preferred_element_type=jnp.float32)
    queries = (projected[0] + q_bias).astype(jnp.bfloat16)
    key_rows = projected[1].astype(jnp.bfloat16)
    value_rows = (projected[2] + v_bias).astype(jnp.bfloat16)
    q_blocks = queries.reshape(clip_count, block_len, shard_local_width)
    key_values = jnp.concatenate([key_rows, value_rows], -1)
    key_values = kv_gather(
        key_values.reshape(clip_count, block_len, 2 * shard_local_width)
    )
    attn_blocks, attn_cols, log_norm = attend(q_blocks, key_values)
    attn_low = attn_blocks.reshape(count_of_rows, shard_local_width)
    attn_term = jnp.dot(attn_low, wout_full, preferred_element_type=jnp.float32)
    residual = x_rows + tp_total(attn_term) + out_bias
    normed_two, unit_two, inv_two = norm_rows(residual, ln2_gain, ln2_bias)
    act_two = normed_two.astype(jnp.bfloat16)
    hidden_pre = jnp.dot(act_two, wup_full, preferred_element_type=jnp.float32) + up_bias
    hidden = jax.nn.gelu(hidden_pre, approximate=False).astype(jnp.bfloat16)
    branch_term = jnp.dot(hidden, wdown_full, preferred_element_type=jnp.float32)
    grad_y = cotangent.astype(jnp.float32).reshape(count_of_rows, model_width)
    grad_db = jnp.sum(rows_part(grad_y), 0)
    grad_ylow = grad_y.astype(jnp.bfloat16)
    grad_wdown = jnp.einsum("rf,rd->fd", hidden, grad_ylow, preferred_element_type=jnp.float32)
    grad_hidden = jnp.einsum("rd,fd->rf", grad_ylow, wdown_full, preferred_element_type=jnp.float32)
    grad_pre = (grad_hidden * gelu_slope(hidden_pre)).astype(jnp.bfloat16)
    grad_ub = jnp.sum(grad_pre.astype(jnp.float32), 0)
    grad_wup = jnp.einsum("rd,rf->df", act_two, grad_pre, preferred_element_type=jnp.float32)
    acttwo_term = jnp.einsum("rf,df->rd", grad_pre, wup_full, preferred_element_type=jnp.float32)
    grad_acttwo = lax.psum(acttwo_term.astype(jnp.bfloat16), "tp")
    owned_up, owned_down = hidden_totals(grad_wup, grad_wdown)
    grad_acttwo, branch_term, owned_up, owned_down = lax.optimization_barrier(
        (grad_acttwo, branch_term.astype(jnp.bfloat16), owned_up, owned_down)
    )
    grad_acttwo = grad_acttwo.astype(jnp.float32)
    branch_total = lax.psum(branch_term, "tp").astype(jnp.float32)
    output = (
        (residual + branch_total + down_bias)
        .astype(jnp.bfloat16)
        .reshape(clip_count, block_len, model_width)
    )
    grad_resid = grad_y + norm_back(grad_acttwo, unit_two, inv_two, ln2_gain)
    grad_g2 = jnp.sum(rows_part(grad_acttwo) * rows_part(unit_two), 0)
    grad_b2 = jnp.sum(rows_part(grad_acttwo), 0)
    grad_ob = jnp.sum(rows_part(grad_resid), 0)
    grad_mixed = grad_resid.astype(jnp.bfloat16)
    grad_wout = jnp.einsum("rc,rd->cd", attn_low, grad_mixed, preferred_element_type=jnp.float32)
    grad_attn = jnp.einsum(
        "rd,cd->rc", grad_mixed, wout_full, preferred_element_type=jnp.float32
    ).astype(jnp.bfloat16)
    grad_query, grad_kv = attend_back(
        q_blocks,
        key_values,
        grad_attn.reshape(clip_count, block_len, shard_local_width),
        attn_cols,
        log_norm,
    )
    key_value_totals = kv_scatter(grad_kv)
    key_value_totals = key_value_totals.reshape(count_of_rows, 2 * shard_local_width)
    query_gradient_partial = grad_query.reshape(count_of_rows, shard_local_width)
    key_gradient_partial = key_value_totals[:, :shard_local_width]
    value_gradient_partial = key_value_totals[:, shard_local_width:]
    three = (query_gradient_partial, key_gradient_partial, value_gradient_partial)
    grad_qb = jnp.sum(query_gradient_partial.astype(jnp.float32), 0)
    grad_vb = jnp.sum(value_gradient_partial.astype(jnp.float32), 0)
    grad_three = [
        jnp.einsum("rd,rc->dc", act_one, part, preferred_element_type=jnp.float32) for part in three
    ]
    actone_term = sum(
        jnp.einsum("rc,dc->rd", part, wqkv_full[i], preferred_element_type=jnp.float32)
        for i, part in enumerate(three)
    )
    actone_term, output = lax.optimization_barrier((actone_term, output))
    grad_actone = lax.psum(actone_term.astype(jnp.bfloat16), "tp")
    owned_qkv, owned_out = mixer_totals(grad_three, grad_wout)
    grad_actone, owned_qkv, owned_out = lax.optimization_barrier(
        (grad_actone, owned_qkv, owned_out)
    )
    grad_actone = grad_actone.astype(jnp.float32)
    input_norm = norm_back(grad_actone, unit_one, inv_one, ln1_gain)
    grad_g1 = jnp.sum(rows_part(grad_actone) * rows_part(unit_one), 0)
    grad_b1 = jnp.sum(rows_part(grad_actone), 0)
    grad_inputs = (
        (grad_resid + input_norm).astype(jnp.bfloat16).reshape(clip_count, block_len, model_width)
    )
    owned = (owned_qkv, owned_out, owned_up, owned_down)
    norm_rows_six = jnp.stack([grad_g1, grad_b1, grad_ob, grad_g2, grad_b2, grad_db])
    hidden_width = grad_ub.shape[0]
    if hidden_width == model_width and 2 * shard_local_width <= model_width:
        pad = jnp.zeros((model_width - 2 * shard_local_width,), jnp.float32)
        packed = jnp.concatenate(
            [
                norm_rows_six,
                jnp.zeros((2, model_width), jnp.float32),
                grad_ub[None],
                jnp.concatenate([grad_qb, grad_vb, pad])[None],
                jnp.zeros((6, model_width), jnp.float32),
            ]
        )
        summed = small_sums(packed, 8)
        norm_sums = summed[:6]
        vectors = (
            summed[9, :shard_local_width],
            summed[9, shard_local_width : 2 * shard_local_width],
            summed[8],
        )
    else:
        vectors = lax.psum((grad_qb, grad_vb, grad_ub), ("shard", "ctx"))
        norm_sums = lax.psum(norm_rows_six, ("shard", "ctx", "tp"))
    return (
        output,
        grad_inputs,
        norm_sums[0],
        norm_sums[1],
        owned[0],
        vectors[0],
        vectors[1],
        owned[1],
        norm_sums[2],
        norm_sums[3],
        norm_sums[4],
        owned[2],
        vectors[2],
        owned[3],
        norm_sums[5],
    )


def solution(mesh):
    placed = (
        P("shard", "ctx", None),
        P("shard", "ctx", None),
        P(),
        P(),
        P(None, "shard", "tp"),
        P("tp"),
        P("tp"),
        P("tp", "shard"),
        P(),
        P(),
        P(),
        P("shard", "tp"),
        P("tp"),
        P("tp", "shard"),
        P(),
    )
    return jax.shard_map(
        shards,
        mesh=mesh,
        in_specs=placed,
        out_specs=(
            P("shard", "ctx", None),
            P("shard", "ctx", None),
            P(),
            P(),
            P(None, "shard", "tp"),
            P("tp"),
            P("tp"),
            P("tp", "shard"),
            P(),
            P(),
            P(),
            P("shard", "tp"),
            P("tp"),
            P("tp", "shard"),
            P(),
        ),
        check_vma=False,
    )
```

```python
import functools

import jax
import jax.numpy as jnp
from jax import lax
from jax.experimental import pallas as pl
from jax.experimental.pallas import tpu as pltpu
from jax.sharding import PartitionSpec as P

HEAD_DIM = 64


norm_eps = 1e-05
inv_root_two = 0.7071067811865476
inv_root_tau = 0.3989422804014327


def norm_rows(inputs_f, gain_vec, bias_vec):
    row_mean = jnp.mean(inputs_f, -1, keepdims=True)
    centred = inputs_f - row_mean
    row_var = jnp.mean(centred * centred, -1, keepdims=True)
    inv_std = lax.rsqrt(row_var + norm_eps)
    unit_rows = centred * inv_std
    return (unit_rows * gain_vec + bias_vec, unit_rows, inv_std)


def norm_back(upstream, unit_rows, inv_std, gain_vec):
    scaled = upstream * gain_vec
    inner = (
        scaled
        - jnp.mean(scaled, -1, keepdims=True)
        - unit_rows * jnp.mean(scaled * unit_rows, -1, keepdims=True)
    )
    return inv_std * inner


def gelu_slope(pre_act):
    cumulative = 0.5 * (1.0 + lax.erf(pre_act * inv_root_two))
    density = jnp.exp(-0.5 * pre_act * pre_act) * inv_root_tau
    return cumulative + pre_act * density


MESH = pl.DeviceIdType.MESH
ROW_DIMS = (((0,), (0,)), ((), ()))
LAST_DIMS = (((1,), (1,)), ((), ()))
VMEM_BYTES = 50 * 1024 * 1024


def scores_of(q_ref, kv_ref, head, width):
    cols = slice(head * HEAD_DIM, (head + 1) * HEAD_DIM)
    vcols = slice(width + head * HEAD_DIM, width + (head + 1) * HEAD_DIM)
    blocks, _, block_len, _ = kv_ref.shape
    q = q_ref[0, :, cols] * jnp.bfloat16(HEAD_DIM**-0.5)
    k = kv_ref[:, 0, :, cols].reshape(blocks * block_len, HEAD_DIM)
    v = kv_ref[:, 0, :, vcols].reshape(blocks * block_len, HEAD_DIM)
    s = lax.dot_general(k, q, LAST_DIMS, preferred_element_type=jnp.float32)
    return q, k, v, s


def attend_kernel(q_ref, kv_ref, o_ref, ot_ref, lse_ref):
    width = q_ref.shape[2]
    for head in range(width // HEAD_DIM):
        q, k, v, s = scores_of(q_ref, kv_ref, head, width)
        top = jnp.max(s, 0, keepdims=True)
        e = jnp.exp(s - top)
        total = jnp.sum(e, 0, keepdims=True)
        ot = lax.dot_general(
            v, e.astype(jnp.bfloat16), ROW_DIMS, preferred_element_type=jnp.float32
        )
        ot_ref[0, head * HEAD_DIM : (head + 1) * HEAD_DIM, :] = ot / total
        lse_ref[0, head : head + 1, :] = top + jnp.log(total)
    o_ref[0] = ot_ref[0].T.astype(jnp.bfloat16)


def attend(q, kv):
    clips, length, width = q.shape
    blocks = kv.shape[0]
    heads = width // HEAD_DIM
    work = clips * heads * length * blocks * length
    row = pl.BlockSpec((1, length, width), lambda c: (c, 0, 0))
    return pl.pallas_call(
        attend_kernel,
        grid=(clips,),
        in_specs=[row, pl.BlockSpec((blocks, 1, length, 2 * width), lambda c: (0, c, 0, 0))],
        out_specs=[
            row,
            pl.BlockSpec((1, width, length), lambda c: (c, 0, 0)),
            pl.BlockSpec((1, 8, length), lambda c: (c, 0, 0)),
        ],
        out_shape=[
            jax.ShapeDtypeStruct(q.shape, jnp.bfloat16),
            jax.ShapeDtypeStruct((clips, width, length), jnp.float32),
            jax.ShapeDtypeStruct((clips, 8, length), jnp.float32),
        ],
        compiler_params=pltpu.CompilerParams(vmem_limit_bytes=VMEM_BYTES),
        cost_estimate=pl.CostEstimate(
            flops=4 * work * HEAD_DIM, bytes_accessed=4 * q.size * 5, transcendentals=work
        ),
    )(q, kv)


def attend_back_kernel(q_ref, kv_ref, do_ref, ot_ref, lse_ref, dq_ref, dkv_ref, dqt_ref):
    width = q_ref.shape[2]
    blocks, _, block_len, _ = kv_ref.shape
    scale = HEAD_DIM**-0.5
    dot_all = do_ref[0].astype(jnp.float32).T
    for head in range(width // HEAD_DIM):
        cols = slice(head * HEAD_DIM, (head + 1) * HEAD_DIM)
        vcols = slice(width + head * HEAD_DIM, width + (head + 1) * HEAD_DIM)
        q, k, v, s = scores_of(q_ref, kv_ref, head, width)
        do = do_ref[0, :, cols]
        delta = jnp.sum(dot_all[cols, :] * ot_ref[0, cols, :], 0, keepdims=True)
        p = jnp.exp(s - lse_ref[0, head : head + 1, :])
        dp = lax.dot_general(v, do, LAST_DIMS, preferred_element_type=jnp.float32)
        ds = (p * (dp - delta)).astype(jnp.bfloat16)
        dv = jnp.dot(p.astype(jnp.bfloat16), do, preferred_element_type=jnp.float32)
        dk = jnp.dot(ds, q, preferred_element_type=jnp.float32)
        dqt_ref[cols, :] = (
            lax.dot_general(k, ds, ROW_DIMS, preferred_element_type=jnp.float32) * scale
        )
        dkv_ref[:, 0, :, cols] = dk.astype(jnp.bfloat16).reshape(blocks, block_len, HEAD_DIM)
        dkv_ref[:, 0, :, vcols] = dv.astype(jnp.bfloat16).reshape(blocks, block_len, HEAD_DIM)
    dq_ref[0] = dqt_ref[...].T.astype(jnp.bfloat16)


def attend_back(q, kv, do, ot, lse):
    clips, length, width = q.shape
    blocks = kv.shape[0]
    heads = width // HEAD_DIM
    work = clips * heads * length * blocks * length
    row = pl.BlockSpec((1, length, width), lambda c: (c, 0, 0))
    wide = pl.BlockSpec((blocks, 1, length, 2 * width), lambda c: (0, c, 0, 0))
    return pl.pallas_call(
        attend_back_kernel,
        grid=(clips,),
        in_specs=[
            row,
            wide,
            row,
            pl.BlockSpec((1, width, length), lambda c: (c, 0, 0)),
            pl.BlockSpec((1, 8, length), lambda c: (c, 0, 0)),
        ],
        out_specs=[row, wide],
        out_shape=[
            jax.ShapeDtypeStruct(q.shape, jnp.bfloat16),
            jax.ShapeDtypeStruct(kv.shape, jnp.bfloat16),
        ],
        scratch_shapes=[pltpu.VMEM((width, length), jnp.float32)],
        compiler_params=pltpu.CompilerParams(vmem_limit_bytes=VMEM_BYTES),
        cost_estimate=pl.CostEstimate(
            flops=10 * work * HEAD_DIM, bytes_accessed=4 * q.size * 10, transcendentals=work
        ),
    )(q, kv, do, ot, lse)


def greet(partners):
    barrier = pltpu.get_barrier_semaphore()
    for partner in partners:
        pl.semaphore_signal(barrier, inc=1, device_id=partner, device_id_type=MESH)
    pl.semaphore_wait(barrier, len(partners))


def remote(src, dst, sems, slot, partner):
    copy = pltpu.make_async_remote_copy(
        src_ref=src,
        dst_ref=dst,
        send_sem=sems[0].at[slot],
        recv_sem=sems[1].at[slot],
        device_id=partner,
        device_id_type=MESH,
    )
    copy.start()
    return copy


def places():
    shard, ctx, tp = lax.axis_index("shard"), lax.axis_index("ctx"), lax.axis_index("tp")
    side, core = ctx // 2, ctx % 2
    by_core = (shard, side * 2 + 1 - core, tp)
    by_shard = (1 - shard, ctx, tp)
    by_side = (shard, (1 - side) * 2 + core, tp)
    return shard, side, core, by_core, by_shard, by_side


def in_pairs():
    return lax.axis_size("shard") == 2 and lax.axis_size("ctx") == 4


def piece_of(ref, shard, core):
    if len(ref.shape) == 4:
        return ref.at[shard, core]
    half = ref.shape[2] // 2
    return ref.at[core, :, pl.ds(pl.multiple_of(shard * half, half), half)]


def piece_shape(part):
    if part.ndim == 4:
        return part.shape[2:]
    return (part.shape[1], part.shape[2] // 2)


def wide_f32(ref):
    return ref[...].astype(jnp.float32)


def owner_sums_kernel(count, *refs):
    parts, outs, rest = refs[:count], refs[count : 2 * count], refs[2 * count :]
    per = 7
    scratch = [rest[per * i : per * (i + 1)] for i in range(count)]
    sems = rest[per * count :]
    shard, side, core, by_core, by_shard, by_side = places()
    greet((by_core, by_shard, by_side))
    first = []
    for i in range(count):
        for slot, owner in enumerate((1 - shard, shard)):
            first.append(
                remote(
                    piece_of(parts[i], owner, 1 - core),
                    scratch[i][0].at[slot],
                    sems,
                    5 * i + slot,
                    by_core,
                )
            )
    second, third, fourth = [], [], []
    for i in range(count):
        in_one, send_two, in_two, send_three, in_three, send_four, in_four = scratch[i]
        first[2 * i].wait()
        send_two[...] = (
            wide_f32(piece_of(parts[i], 1 - shard, core)) + wide_f32(in_one.at[0])
        ).astype(jnp.bfloat16)
        second.append(remote(send_two, in_two, sems, 5 * i + 2, by_shard))
    for i in range(count):
        in_one, send_two, in_two, send_three, in_three, send_four, in_four = scratch[i]
        first[2 * i + 1].wait()
        second[i].wait()
        send_three[...] = (
            wide_f32(piece_of(parts[i], shard, core)) + wide_f32(in_one.at[1]) + wide_f32(in_two)
        ).astype(jnp.bfloat16)
        third.append(remote(send_three, in_three, sems, 5 * i + 3, by_side))
    for i in range(count):
        in_one, send_two, in_two, send_three, in_three, send_four, in_four = scratch[i]
        third[i].wait()
        send_four[...] = (wide_f32(send_three) + wide_f32(in_three)).astype(jnp.bfloat16)
        fourth.append(remote(send_four, in_four, sems, 5 * i + 4, by_core))
        outs[i][core] = wide_f32(send_four)
    for i in range(count):
        fourth[i].wait()
        outs[i][1 - core] = wide_f32(scratch[i][6])


def owner_sums(parts, collective):
    scratch = []
    for part in parts:
        shape = piece_shape(part)
        scratch += [pltpu.VMEM((2,) + shape, jnp.bfloat16)]
        scratch += [pltpu.VMEM(shape, jnp.bfloat16)] * 6
    count = len(parts)
    size = sum(part.size for part in parts)
    vmem = pl.BlockSpec(memory_space=pltpu.VMEM)
    return pl.pallas_call(
        functools.partial(owner_sums_kernel, count),
        in_specs=[vmem] * count,
        out_specs=[vmem] * count,
        out_shape=[jax.ShapeDtypeStruct((2,) + piece_shape(part), jnp.float32) for part in parts],
        scratch_shapes=scratch + [pltpu.SemaphoreType.DMA((5 * count,))] * 2,
        compiler_params=pltpu.CompilerParams(
            collective_id=collective, has_side_effects=True, vmem_limit_bytes=VMEM_BYTES
        ),
        cost_estimate=pl.CostEstimate(flops=size, bytes_accessed=size * 30, transcendentals=0),
    )(*parts)


def kv_gather_kernel(own_ref, all_ref, send_sem, recv_sem):
    shard, side, core, by_core, by_shard, by_side = places()
    clips = own_ref.shape[0]
    sems = (send_sem, recv_sem)
    mine, across = side * 2 + core, (1 - side) * 2 + core
    greet((by_core, by_side))
    sent = [
        remote(own_ref.at[c], all_ref.at[mine, c], sems, c, by_side) for c in range(clips)
    ]
    near = remote(own_ref, all_ref.at[mine], sems, 2 * clips, by_core)
    all_ref[mine] = own_ref[...]
    passed = []
    for c in range(clips):
        sent[c].wait()
        passed.append(
            remote(all_ref.at[across, c], all_ref.at[across, c], sems, clips + c, by_core)
        )
    near.wait()
    for copy in passed:
        copy.wait()


def kv_gather(own):
    if not in_pairs():
        return lax.all_gather(own, "ctx", axis=0)
    vmem = pl.BlockSpec(memory_space=pltpu.VMEM)
    return pl.pallas_call(
        kv_gather_kernel,
        in_specs=[vmem],
        out_specs=vmem,
        out_shape=jax.ShapeDtypeStruct((4,) + own.shape, own.dtype),
        scratch_shapes=[pltpu.SemaphoreType.DMA((2 * own.shape[0] + 1,))] * 2,
        compiler_params=pltpu.CompilerParams(
            collective_id=8, has_side_effects=True, vmem_limit_bytes=VMEM_BYTES
        ),
        cost_estimate=pl.CostEstimate(flops=0, bytes_accessed=own.size * 80, transcendentals=0),
    )(own)


def kv_scatter_kernel(all_ref, own_ref, in_core, send_side, in_side, send_sem, recv_sem):
    shard, side, core, by_core, by_shard, by_side = places()
    clips = own_ref.shape[0]
    sems = (send_sem, recv_sem)
    greet((by_core, by_side))
    near = [
        remote(
            all_ref.at[owner * 2 + 1 - core, c], in_core.at[slot, c], sems, slot * clips + c, by_core
        )
        for slot, owner in enumerate((1 - side, side))
        for c in range(clips)
    ]
    far = []
    for c in range(clips):
        near[c].wait()
        send_side[c] = (
            wide_f32(all_ref.at[(1 - side) * 2 + core, c]) + wide_f32(in_core.at[0, c])
        ).astype(jnp.bfloat16)
        far.append(remote(send_side.at[c], in_side.at[c], sems, 2 * clips + c, by_side))
    for c in range(clips):
        near[clips + c].wait()
        far[c].wait()
        own_ref[c] = (
            wide_f32(all_ref.at[side * 2 + core, c])
            + wide_f32(in_core.at[1, c])
            + wide_f32(in_side.at[c])
        ).astype(jnp.bfloat16)


def kv_scatter(parts):
    if not in_pairs():
        return lax.psum_scatter(parts, "ctx", scatter_dimension=0, tiled=False)
    vmem = pl.BlockSpec(memory_space=pltpu.VMEM)
    own = parts.shape[1:]
    return pl.pallas_call(
        kv_scatter_kernel,
        in_specs=[vmem],
        out_specs=vmem,
        out_shape=jax.ShapeDtypeStruct(own, parts.dtype),
        scratch_shapes=[
            pltpu.VMEM((2,) + own, jnp.bfloat16),
            pltpu.VMEM(own, jnp.bfloat16),
            pltpu.VMEM(own, jnp.bfloat16),
        ]
        + [pltpu.SemaphoreType.DMA((3 * own[0],))] * 2,
        compiler_params=pltpu.CompilerParams(
            collective_id=9, has_side_effects=True, vmem_limit_bytes=VMEM_BYTES
        ),
        cost_estimate=pl.CostEstimate(flops=0, bytes_accessed=parts.size * 25, transcendentals=0),
    )(parts)


def weight_gather_kernel(qkv_ref, out_ref, qkv_all, out_all, send_sem, recv_sem):
    shard, side, core, by_core, by_shard, by_side = places()
    sems = (send_sem, recv_sem)
    half, part = qkv_ref.shape[1] // 2, out_ref.shape[0] // 2
    cols = out_ref.shape[1]

    def qkv_slot(owner):
        return qkv_all.at[:, owner, pl.ds(pl.multiple_of(core * half, half), half), :]

    def out_slot(owner):
        return out_all.at[
            pl.ds(pl.multiple_of(core * part, part), part),
            pl.ds(pl.multiple_of(owner * cols, cols), cols),
        ]

    greet((by_core, by_shard))
    sent = [
        remote(
            qkv_ref.at[:, pl.ds(pl.multiple_of(core * half, half), half), :],
            qkv_slot(shard),
            sems,
            0,
            by_shard,
        ),
        remote(
            out_ref.at[pl.ds(pl.multiple_of(core * part, part), part), :],
            out_slot(shard),
            sems,
            1,
            by_shard,
        ),
    ]
    qkv_all[:, shard] = qkv_ref[...]
    out_all[:, pl.ds(pl.multiple_of(shard * cols, cols), cols)] = out_ref[...]
    sent[0].wait()
    passed = [remote(qkv_slot(1 - shard), qkv_slot(1 - shard), sems, 2, by_core)]
    sent[1].wait()
    passed.append(remote(out_slot(1 - shard), out_slot(1 - shard), sems, 3, by_core))
    for copy in passed:
        copy.wait()


def weight_gather(w_qkv, w_out):
    if not in_pairs():
        return (
            lax.all_gather(w_qkv, "shard", axis=1, tiled=True),
            lax.all_gather(w_out, "shard", axis=1, tiled=True),
        )
    three, rows, local = w_qkv.shape
    vmem = pl.BlockSpec(memory_space=pltpu.VMEM)
    qkv, out = pl.pallas_call(
        weight_gather_kernel,
        in_specs=[vmem, vmem],
        out_specs=[vmem, vmem],
        out_shape=[
            jax.ShapeDtypeStruct((three, 2, rows, local), w_qkv.dtype),
            jax.ShapeDtypeStruct((local, 2 * rows), w_out.dtype),
        ],
        scratch_shapes=[pltpu.SemaphoreType.DMA((4,))] * 2,
        compiler_params=pltpu.CompilerParams(
            collective_id=10, has_side_effects=True, vmem_limit_bytes=VMEM_BYTES
        ),
        cost_estimate=pl.CostEstimate(flops=0, bytes_accessed=w_qkv.size * 60, transcendentals=0),
    )(w_qkv, w_out)
    return qkv.reshape(three, 2 * rows, local), out


def small_sums_kernel(rows_all, vec_ref, out_ref, plane_in, line_out, line_in, sems_a, sems_b):
    shard, ctx, tp = lax.axis_index("shard"), lax.axis_index("ctx"), lax.axis_index("tp")
    n_shard, n_ctx, n_tp = (lax.axis_size(a) for a in ("shard", "ctx", "tp"))
    plane = n_shard * n_ctx
    me = shard * n_ctx + ctx
    partners = []
    for step in range(1, plane):
        other = lax.rem(me + step, plane)
        partners.append((other // n_ctx, lax.rem(other, n_ctx), tp))
    lines = [(shard, ctx, lax.rem(tp + step, n_tp)) for step in range(1, n_tp)]
    greet(partners + lines)
    copies = [
        remote(vec_ref, plane_in.at[step], (sems_a.at[0], sems_a.at[1]), step, partners[step])
        for step in range(plane - 1)
    ]
    for copy in copies:
        copy.wait()
    total = jnp.zeros_like(vec_ref[...])
    for source in range(plane):
        gap = lax.rem(me - source + plane, plane)
        slot = jnp.maximum(gap - 1, 0)
        total += jnp.where(gap == 0, vec_ref[...], plane_in[slot])
    line_out[...] = total[:rows_all]
    copies = [
        remote(line_out, line_in.at[step], (sems_b.at[0], sems_b.at[1]), step, lines[step])
        for step in range(n_tp - 1)
    ]
    if rows_all < vec_ref.shape[0]:
        out_ref[rows_all:] = total[rows_all:]
    for copy in copies:
        copy.wait()
    total = jnp.zeros_like(line_out[...])
    for source in range(n_tp):
        gap = lax.rem(tp - source + n_tp, n_tp)
        slot = jnp.maximum(gap - 1, 0)
        total += jnp.where(gap == 0, line_out[...], line_in[slot])
    out_ref[:rows_all] = total


def small_sums(vec, rows_all, collective):
    plane = lax.axis_size("shard") * lax.axis_size("ctx")
    n_tp = lax.axis_size("tp")
    vmem = pl.BlockSpec(memory_space=pltpu.VMEM)
    low = (rows_all, vec.shape[1])
    return pl.pallas_call(
        functools.partial(small_sums_kernel, rows_all),
        in_specs=[vmem],
        out_specs=vmem,
        out_shape=jax.ShapeDtypeStruct(vec.shape, jnp.float32),
        scratch_shapes=[
            pltpu.VMEM((plane - 1,) + vec.shape, jnp.float32),
            pltpu.VMEM(low, jnp.float32),
            pltpu.VMEM((n_tp - 1,) + low, jnp.float32),
            pltpu.SemaphoreType.DMA((2, plane - 1)),
            pltpu.SemaphoreType.DMA((2, n_tp - 1)),
        ],
        compiler_params=pltpu.CompilerParams(
            collective_id=collective, has_side_effects=True, vmem_limit_bytes=VMEM_BYTES
        ),
        cost_estimate=pl.CostEstimate(flops=vec.size, bytes_accessed=vec.size * 40, transcendentals=0),
    )(vec)


def tp_total(values):
    return lax.psum(values.astype(jnp.bfloat16), "tp").astype(jnp.float32)


def plain_totals(grad, dim):
    part = lax.psum_scatter(grad, "shard", scatter_dimension=dim, tiled=True)
    return lax.psum(part, "ctx").astype(jnp.float32)


def hidden_totals(grad_wup, grad_wdown):
    up, down = grad_wup.astype(jnp.bfloat16), grad_wdown.astype(jnp.bfloat16)
    if not in_pairs():
        return plain_totals(up, 0), plain_totals(down, 1)
    width, hidden = up.shape
    up, down = owner_sums(
        (up.reshape(2, 2, width // 4, hidden), down.reshape(2, hidden // 2, width)), 3
    )
    return up.reshape(width // 2, hidden), down.reshape(hidden, width // 2)


def mixer_totals(grad_three, grad_wout):
    three = [g.astype(jnp.bfloat16) for g in grad_three]
    out = grad_wout.astype(jnp.bfloat16)
    if not in_pairs():
        return plain_totals(jnp.stack(three), 1), plain_totals(out, 1)
    local, width = out.shape
    sums = owner_sums(
        tuple(g.reshape(2, 2, width // 4, local) for g in three)
        + (out.reshape(2, local // 2, width),),
        4,
    )
    qkv = jnp.stack([g.reshape(width // 2, local) for g in sums[:3]])
    return qkv, sums[3].reshape(local, width // 2)


def late_sums(rows):
    if not in_pairs():
        return lax.psum(rows, ("shard", "ctx", "tp"))
    return small_sums(rows, rows.shape[0], 7)


def early_sums(rows, vectors):
    q_vec, v_vec, up_vec = vectors
    model_width, local = rows.shape[1], q_vec.shape[0]
    if not in_pairs() or up_vec.shape[0] != model_width or 2 * local > model_width:
        return lax.psum(rows, ("shard", "ctx", "tp")), lax.psum(vectors, ("shard", "ctx"))
    pad = jnp.zeros((model_width - 2 * local,), jnp.float32)
    packed = jnp.concatenate(
        [
            rows,
            jnp.zeros((4, model_width), jnp.float32),
            up_vec[None],
            jnp.concatenate([q_vec, v_vec, pad])[None],
            jnp.zeros((6, model_width), jnp.float32),
        ]
    )
    summed = small_sums(packed, 8, 11)
    return summed[:4], (summed[9, :local], summed[9, local : 2 * local], summed[8])


def shards(
    inputs,
    cotangent,
    ln1_gain,
    ln1_bias,
    w_qkv,
    q_bias,
    v_bias,
    w_out,
    out_bias,
    ln2_gain,
    ln2_bias,
    w_up,
    up_bias,
    w_down,
    down_bias,
):
    clip_count, block_len, model_width = inputs.shape
    count_of_rows = clip_count * block_len
    share_rows = count_of_rows // lax.axis_size("tp")
    share_start = lax.axis_index("tp") * share_rows

    def rows_part(values):
        return lax.dynamic_slice_in_dim(values, share_start, share_rows, 0)

    wqkv_full, wout_full = weight_gather(w_qkv, w_out)
    wup_full, wdown_full = (
        lax.all_gather(w_up, "shard", axis=0, tiled=True),
        lax.all_gather(w_down, "shard", axis=1, tiled=True),
    )
    shard_local_width = wqkv_full.shape[2]
    x_rows = inputs.astype(jnp.float32).reshape(count_of_rows, model_width)
    normed_one, unit_one, inv_one = norm_rows(x_rows, ln1_gain, ln1_bias)
    act_one = normed_one.astype(jnp.bfloat16)
    projected = jnp.einsum("rd,kdc->krc", act_one, wqkv_full, preferred_element_type=jnp.float32)
    queries = (projected[0] + q_bias).astype(jnp.bfloat16)
    key_rows = projected[1].astype(jnp.bfloat16)
    value_rows = (projected[2] + v_bias).astype(jnp.bfloat16)
    q_blocks = queries.reshape(clip_count, block_len, shard_local_width)
    key_values = jnp.concatenate([key_rows, value_rows], -1)
    key_values = kv_gather(
        key_values.reshape(clip_count, block_len, 2 * shard_local_width)
    )
    attn_blocks, attn_cols, log_norm = attend(q_blocks, key_values)
    attn_low = attn_blocks.reshape(count_of_rows, shard_local_width)
    attn_term = jnp.dot(attn_low, wout_full, preferred_element_type=jnp.float32)
    residual = x_rows + tp_total(attn_term) + out_bias
    normed_two, unit_two, inv_two = norm_rows(residual, ln2_gain, ln2_bias)
    act_two = normed_two.astype(jnp.bfloat16)
    hidden_pre = jnp.dot(act_two, wup_full, preferred_element_type=jnp.float32) + up_bias
    hidden = jax.nn.gelu(hidden_pre, approximate=False).astype(jnp.bfloat16)
    branch_term = jnp.dot(hidden, wdown_full, preferred_element_type=jnp.float32)
    grad_y = cotangent.astype(jnp.float32).reshape(count_of_rows, model_width)
    grad_db = jnp.sum(rows_part(grad_y), 0)
    grad_ylow = grad_y.astype(jnp.bfloat16)
    grad_wdown = jnp.einsum("rf,rd->fd", hidden, grad_ylow, preferred_element_type=jnp.float32)
    grad_hidden = jnp.einsum("rd,fd->rf", grad_ylow, wdown_full, preferred_element_type=jnp.float32)
    grad_pre = (grad_hidden * gelu_slope(hidden_pre)).astype(jnp.bfloat16)
    grad_ub = jnp.sum(grad_pre.astype(jnp.float32), 0)
    grad_wup = jnp.einsum("rd,rf->df", act_two, grad_pre, preferred_element_type=jnp.float32)
    acttwo_term = jnp.einsum("rf,df->rd", grad_pre, wup_full, preferred_element_type=jnp.float32)
    grad_acttwo = lax.psum(acttwo_term.astype(jnp.bfloat16), "tp")
    owned_up, owned_down = hidden_totals(grad_wup, grad_wdown)
    grad_acttwo, branch_term, owned_up, owned_down = lax.optimization_barrier(
        (grad_acttwo, branch_term.astype(jnp.bfloat16), owned_up, owned_down)
    )
    grad_acttwo = grad_acttwo.astype(jnp.float32)
    branch_low = lax.psum(branch_term, "tp")
    grad_resid = grad_y + norm_back(grad_acttwo, unit_two, inv_two, ln2_gain)
    grad_g2 = jnp.sum(rows_part(grad_acttwo) * rows_part(unit_two), 0)
    grad_b2 = jnp.sum(rows_part(grad_acttwo), 0)
    grad_ob = jnp.sum(rows_part(grad_resid), 0)
    grad_mixed = grad_resid.astype(jnp.bfloat16)
    grad_wout = jnp.einsum("rc,rd->cd", attn_low, grad_mixed, preferred_element_type=jnp.float32)
    grad_attn = jnp.einsum(
        "rd,cd->rc", grad_mixed, wout_full, preferred_element_type=jnp.float32
    ).astype(jnp.bfloat16)
    grad_query, grad_kv = attend_back(
        q_blocks,
        key_values,
        grad_attn.reshape(clip_count, block_len, shard_local_width),
        attn_cols,
        log_norm,
    )
    key_value_totals = kv_scatter(grad_kv)
    key_value_totals = key_value_totals.reshape(count_of_rows, 2 * shard_local_width)
    query_gradient_partial = grad_query.reshape(count_of_rows, shard_local_width)
    key_gradient_partial = key_value_totals[:, :shard_local_width]
    value_gradient_partial = key_value_totals[:, shard_local_width:]
    three = (query_gradient_partial, key_gradient_partial, value_gradient_partial)
    grad_qb = jnp.sum(query_gradient_partial.astype(jnp.float32), 0)
    grad_vb = jnp.sum(value_gradient_partial.astype(jnp.float32), 0)
    grad_three = [
        jnp.einsum("rd,rc->dc", act_one, part, preferred_element_type=jnp.float32) for part in three
    ]
    actone_term = sum(
        jnp.einsum("rc,dc->rd", part, wqkv_full[i], preferred_element_type=jnp.float32)
        for i, part in enumerate(three)
    )
    actone_term, branch_low = lax.optimization_barrier((actone_term.astype(jnp.bfloat16), branch_low))
    branch_total = branch_low.astype(jnp.float32)
    output = (
        (residual + branch_total + down_bias)
        .astype(jnp.bfloat16)
        .reshape(clip_count, block_len, model_width)
    )
    grad_actone = lax.psum(actone_term, "tp")
    owned_qkv, owned_out = mixer_totals(grad_three, grad_wout)
    early, vectors = early_sums(
        jnp.stack([grad_ob, grad_g2, grad_b2, grad_db]), (grad_qb, grad_vb, grad_ub)
    )
    grad_actone, owned_qkv, owned_out, early = lax.optimization_barrier(
        (grad_actone, owned_qkv, owned_out, early)
    )
    grad_actone = grad_actone.astype(jnp.float32)
    input_norm = norm_back(grad_actone, unit_one, inv_one, ln1_gain)
    grad_g1 = jnp.sum(rows_part(grad_actone) * rows_part(unit_one), 0)
    grad_b1 = jnp.sum(rows_part(grad_actone), 0)
    grad_inputs = (
        (grad_resid + input_norm).astype(jnp.bfloat16).reshape(clip_count, block_len, model_width)
    )
    owned = (owned_qkv, owned_out, owned_up, owned_down)
    norm_sums = (*late_sums(jnp.stack([grad_g1, grad_b1])), *early)
    return (
        output,
        grad_inputs,
        norm_sums[0],
        norm_sums[1],
        owned[0],
        vectors[0],
        vectors[1],
        owned[1],
        norm_sums[2],
        norm_sums[3],
        norm_sums[4],
        owned[2],
        vectors[2],
        owned[3],
        norm_sums[5],
    )


def solution(mesh):
    placed = (
        P("shard", "ctx", None),
        P("shard", "ctx", None),
        P(),
        P(),
        P(None, "shard", "tp"),
        P("tp"),
        P("tp"),
        P("tp", "shard"),
        P(),
        P(),
        P(),
        P("shard", "tp"),
        P("tp"),
        P("tp", "shard"),
        P(),
    )
    return jax.shard_map(
        shards,
        mesh=mesh,
        in_specs=placed,
        out_specs=(
            P("shard", "ctx", None),
            P("shard", "ctx", None),
            P(),
            P(),
            P(None, "shard", "tp"),
            P("tp"),
            P("tp"),
            P("tp", "shard"),
            P(),
            P(),
            P(),
            P("shard", "tp"),
            P("tp"),
            P("tp", "shard"),
            P(),
        ),
        check_vma=False,
    )
```
